32 devices in a mesh: group: 2 (over x), row: 16 (over z, y, core).
Axes of the slice: x: 2, y: 2, z: 4, core: 2. Of those that a mesh axis runs over, the one named last changes fastest.
Arguments:
- gram_tiles: bfloat16 [4, 16384, 16384], P('group', 'row'), parts along dimension 0, as said below
- weight_panels: bfloat16 [4, 16384, 128], P('group', 'row'), parts along dimension 0, may hold values from -6 to 6
Outputs:
- merged: float32 [32768, 128], P(('group', 'row')), parts along dimension 0
- residual: float32 [32768, 128], P(('group', 'row')), parts along dimension 0
The draws below stay inside these ranges and needn't reach their ends.
There are 2 independent parts, one for each index of `group`. The reference program is written for one: setup_inputs(seed, part) draws one part's arguments, and reference() takes and returns one part's arrays. A program takes and returns all parts, laid end to end along the dimension named above; each array names one. Nothing has to cross between parts.
Inputs may be any that keep to these rules, and one draw needn't show every extreme that they name: `gram_tiles`: each of the 2 Grams is exactly symmetric.
All inputs are finite; a program needn't handle non-finite values.
Results may differ from the reference program's by a relative error of at most 0.0003.
Values may be sent and summed in bfloat16 or wider, within the bound.
No kernel may reach another device: no remote copies, remote signals or barrier semaphores. Data moves between devices by JAX's collectives and lax.ppermute only.
A program may use at most 320 MiB of HBM per device.

```python
import math
import jax
import jax.numpy as jnp
from jax import lax

D = 16384
COLS = 128
MODELS = 2
ITERS = 2


def draw_gram_tiles(key, part):

    def one_model(model_key):
        key_raw, key_diag, key_scale = jax.random.split(model_key, 3)
        raw_values = jax.random.truncated_normal(key_raw, -4.0, 4.0, (D, D), jnp.float32)
        spread = jax.random.uniform(key_scale, (D,), jnp.float32, 1.0, 1.25)
        symmetric = (raw_values + raw_values.T) * (0.5 / math.sqrt(2.0 * D))
        diagonal_values = jax.random.uniform(key_diag, (D,), jnp.float32, 2.5, 5.0)
        row_ids = lax.broadcasted_iota(jnp.int32, (D, D), 0)
        col_ids = lax.broadcasted_iota(jnp.int32, (D, D), 1)
        core_matrix = jnp.where(row_ids == col_ids, diagonal_values[None, :], symmetric)
        positions = jnp.arange(D, dtype=jnp.float32) / D
        row_scale = jnp.exp(0.5 * math.log(3.0) * positions) * spread
        scale_outer = row_scale[:, None] * row_scale[None, :]
        return (core_matrix * scale_outer).astype(jnp.bfloat16)
    model_keys = jax.random.split(jax.random.fold_in(key, 11), MODELS)
    return lax.map(one_model, model_keys)


def levels(stream_key, shape, cuts, smallest, high):
    def one(axis_at, blocks):
        heights = jax.random.uniform(jax.random.fold_in(jax.random.fold_in(stream_key, 6), axis_at), (blocks,), jnp.float32, smallest / len(cuts), high / len(cuts))
        return jnp.repeat(jnp.exp(heights), shape[axis_at] // blocks).reshape((-1,) + (1,) * (len(shape) - axis_at - 1))

    level = one(*cuts[0])
    for cut in cuts[1:]:
        level = level * one(*cut)
    return level


def normal_values(stream_key, extent, scale, reach, cuts=(), kind=jnp.bfloat16):
    array = jax.random.normal(stream_key, extent, jnp.float32) * scale
    if len(cuts) > 0:
        array = levels(stream_key, extent, cuts, -0.22, 0.18) * array
    return jnp.clip(array, min=-reach, max=reach).astype(kind)


def setup_inputs(seed: int = 0, part: int = 0) -> dict:
    keys = jax.random.split(jax.random.key(seed), 3)
    part_splits = jax.random.split(jax.random.fold_in(keys[2], part), 3)
    gram_tiles = draw_gram_tiles(jax.random.fold_in(jax.random.fold_in(keys[2], part), 71), part)
    weight_panels = normal_values(part_splits[1], (MODELS, D, COLS), 1.0, 6.0, ((1, 16),))
    return dict(gram_tiles=gram_tiles, weight_panels=weight_panels)


def reference(gram_tiles, weight_panels):
    summed = jnp.eye(D, dtype=jnp.float32)
    right = jnp.zeros((D, COLS), jnp.float32)
    for model in range(MODELS):
        summed = summed + gram_tiles[model].astype(jnp.float32)
        right = right + jnp.dot(gram_tiles[model], weight_panels[model], preferred_element_type=jnp.float32)
    operator = summed
    merged = jnp.zeros((D, COLS), jnp.float32)
    cg_residual = right
    direction = right
    norm_now = jnp.sum(cg_residual * cg_residual, axis=0)
    for iteration in range(ITERS):
        applied = jnp.dot(operator, direction, precision=lax.Precision.HIGHEST, preferred_element_type=jnp.float32)
        curvature = jnp.sum(direction * applied, axis=0)
        step_size = norm_now / curvature
        merged = merged + step_size * direction
        cg_residual = cg_residual - step_size * applied
        norm_next = jnp.sum(cg_residual * cg_residual, axis=0)
        direction = cg_residual + (norm_next / norm_now) * direction
        norm_now = norm_next
    return (merged, cg_residual)
```

```python
import functools
import jax
import jax.numpy as jnp
from jax import lax
from jax.experimental import pallas as pl
from jax.experimental.pallas import tpu as pltpu
from jax.sharding import PartitionSpec as P

EXTRA = 16


def split_pair(x):
    hi = x.astype(jnp.bfloat16)
    return hi, (x - hi.astype(jnp.float32)).astype(jnp.bfloat16)


SPAN, LOWEST = 29.75, -14.0


def coded_block(x):
    top = jnp.maximum(jnp.max(jnp.abs(x), axis=0, keepdims=True), 1e-30)
    exponent = jnp.floor(jnp.log2(top)) - 4.0
    factor = jnp.ceil(top * jnp.exp2(-exponent) * (512.0 / SPAN)) * (1.0 / 512.0)
    size = jnp.abs(x) / (factor * jnp.exp2(exponent))
    code = jnp.exp2(size + LOWEST)
    row = lax.broadcasted_iota(jnp.int32, (EXTRA, x.shape[1]), 0)
    return jnp.where(x < 0, -code, code), jnp.where(row == 0, exponent, factor)


def decoded_block(code, extra):
    binade = extra[1:2] * jnp.exp2(extra[0:1])
    size = (jnp.log2(jnp.abs(code)) - LOWEST) * binade
    return jnp.where(code < 0, -size, size)


def product_kernel(cfg, ids_ref, gram_ref, *refs):
    blocks, own, panels, has_total, tail = cfg
    refs = list(refs)
    x_refs = [refs.pop(0) for _ in range(blocks)]
    total_ref = refs.pop(0) if has_total else None
    base_ref = refs.pop(0) if tail == "moments" else None
    out_ref = refs.pop(0)
    more_ref = refs.pop(0) if tail else None
    acc, held = refs
    block, piece = pl.program_id(0), pl.program_id(1)
    models, rows, depth = gram_ref.shape
    cols = out_ref.shape[1]

    @pl.when((block == 0) & (piece == 0))
    def _():
        if has_total:
            acc[:, :cols] = total_ref[...]
        else:
            acc[:, :cols] = jnp.zeros((rows, cols), jnp.float32)
        if not panels:
            acc[:, cols:] = jnp.zeros((rows, cols), jnp.float32)

    for i in range(blocks):
        @pl.when((block == i) & (piece == 0))
        def _(i=i):
            if panels:
                held[...] = x_refs[i][...]
                return
            x = x_refs[i][:rows, :]
            if own and i == 0:
                acc[:, :cols] += x
            else:
                x = decoded_block(x, x_refs[i][rows:, :])
            hi, lo = split_pair(x)
            held[:, :cols] = hi
            held[:, cols:] = lo

    at = pl.ds(pl.multiple_of(piece * depth, depth), depth)
    dot = functools.partial(jnp.dot, preferred_element_type=jnp.float32)
    if panels:
        acc[...] += sum(dot(gram_ref[m], held[m, at, :]) for m in range(models))
    else:
        acc[...] += sum(dot(gram_ref[m], held[at, :]) for m in range(models))

    @pl.when((block == blocks - 1) & (piece == pl.num_programs(1) - 1))
    def _():
        result = acc[...] if panels else acc[:, :cols] + acc[:, cols:]
        out_ref[...] = result
        if tail == "send":
            more_ref[:rows, :], more_ref[rows:, :] = coded_block(result)
        if tail == "moments":
            one, two = base_ref[0], base_ref[1]
            pairs = ((one, one), (one, two), (two, two), (two, result))
            sums = [jnp.sum(a * b, axis=0, keepdims=True) for a, b in pairs]
            more_ref[...] = jnp.concatenate(sums + [jnp.zeros((8 - len(sums), cols), jnp.float32)], axis=0)


def product(gram, ids, xs, total=None, *, own=False, panels=False, tail=None, base=None):
    models, rows, _ = gram.shape
    cols = xs[0].shape[-1]
    blocks = len(xs)
    depth = min(1024, rows)
    pieces = rows // depth
    cfg = (blocks, own, panels, total is not None, tail)
    whole = lambda a: pl.BlockSpec(a.shape, lambda b, k, ids: (0,) * a.ndim)
    inputs = list(xs)
    if total is not None:
        inputs.append(total)
    if tail == "moments":
        inputs.append(base)
    outs = [jax.ShapeDtypeStruct((rows, cols), jnp.float32)]
    if tail == "send":
        outs.append(jax.ShapeDtypeStruct((rows + EXTRA, cols), jnp.float32))
    if tail == "moments":
        outs.append(jax.ShapeDtypeStruct((8, cols), jnp.float32))
    width = cols if panels else 2 * cols
    held = (models, rows, cols) if panels else (rows, 2 * cols)
    result = pl.pallas_call(
        functools.partial(product_kernel, cfg),
        out_shape=outs,
        grid_spec=pltpu.PrefetchScalarGridSpec(
            num_scalar_prefetch=1,
            grid=(blocks, pieces),
            in_specs=[
                pl.BlockSpec((models, rows, depth), lambda b, k, ids: (0, 0, ids[b] * pieces + k))
            ] + [whole(a) for a in inputs],
            out_specs=[whole(o) for o in outs],
            scratch_shapes=[
                pltpu.VMEM((rows, width), jnp.float32),
                pltpu.VMEM(held, jnp.bfloat16),
            ],
        ),
        compiler_params=pltpu.CompilerParams(
            dimension_semantics=("arbitrary", "arbitrary"), vmem_limit_bytes=40 * 1024 * 1024
        ),
        cost_estimate=pl.CostEstimate(
            flops=2 * models * rows * rows * blocks * width,
            bytes_accessed=2 * models * rows * rows * blocks,
            transcendentals=0,
        ),
    )(ids, gram, *inputs)
    return result if tail else result[0]


def on_device(devices, gram, panel_rows):
    models, rows, _ = gram.shape
    cols = panel_rows.shape[2]
    chips = devices // 2
    order = list(range(0, chips, 2)) + list(range(chips - 1, 0, -2))
    place_of = [order.index(c) for c in range(chips)]

    def ring(step):
        return [
            (2 * c + core, 2 * order[(j + step) % chips] + core)
            for j, c in enumerate(order) for core in range(2)
        ]

    onward, back = ring(1), ring(-1)
    pair = [(i, i ^ 1) for i in range(devices)]
    send = lambda x, perm: lax.ppermute(x, "row", perm)
    me = lax.axis_index("row")
    core = lax.rem(me, 2)
    chip = me // 2
    place = jnp.where(lax.rem(chip, 2) == 0, chip // 2, chips - 1 - chip // 2)

    def device_at(place):
        place = lax.rem(place + 2 * chips, chips)
        return 2 * jnp.where(place < chips // 2, 2 * place, 2 * (chips - 1 - place) + 1)

    def ids_of(places):
        base = jnp.stack([device_at(p) for p in places])
        return jnp.concatenate([base + core, base + 1 - core]).astype(jnp.int32)

    ids_own = jnp.stack([me, me + 1 - 2 * core]).astype(jnp.int32)

    def gathered(own_block, sent, axis, cut, widen, *, own, panels, tail, base=None):
        call = functools.partial(product, gram, panels=panels)
        beside = send(sent, pair)
        ahead, behind = send(sent, onward), send(sent, back)
        total = call(ids_own, [own_block, widen(beside)], own=own)
        for step in range(1, chips // 2):
            ahead, behind, total = lax.optimization_barrier((ahead, behind, total))
            across = [send(ahead, pair), send(behind, pair)]
            blocks = [widen(x) for x in [ahead, behind] + across]
            if step + 1 < chips // 2:
                ahead, behind = send(ahead, onward), send(behind, back)
            else:
                first = send(lax.slice_in_dim(ahead, 0, cut, axis=axis), onward)
                second = send(lax.slice_in_dim(behind, cut, None, axis=axis), back)
            total = call(ids_of([place - step, place + step]), blocks, total)
        first, second, total = lax.optimization_barrier((first, second, total))
        far = jnp.concatenate([first, second], axis=axis)
        return call(
            ids_of([place + chips // 2]), [widen(far), widen(send(far, pair))], total, tail=tail, base=base
        )

    def vector_stage(x, scaled, **kw):
        return gathered(
            x, scaled.astype(jnp.float16), 0, rows // 2, lambda y: y.astype(jnp.float32),
            own=True, panels=False, **kw
        )

    right, scaled = gathered(
        panel_rows, panel_rows, 1, rows // 2, lambda y: y, own=False, panels=True, tail="send"
    )
    first, scaled = vector_stage(right, scaled, tail="send")
    second, sums = vector_stage(first, scaled, tail="moments", base=jnp.stack([right, first]))

    if devices & (devices - 1):
        sums = lax.psum(sums, "row")
    else:
        bit = 1
        while bit < devices:
            masks = [1, 2, 3] if bit == 1 and devices > 2 else [bit]
            sums = sum([send(sums, [(i, i ^ m) for i in range(devices)]) for m in masks], sums)
            bit *= len(masks) + 1

    norm_now, along, square, cube = (sums[i : i + 1] for i in range(4))
    step_one = norm_now / along
    norm_next = norm_now - 2.0 * step_one * along + step_one * step_one * square
    ratio = norm_next / norm_now
    lead = 1.0 + ratio
    curvature = lead * lead * along - 2.0 * lead * step_one * square + step_one * step_one * cube
    step_two = norm_next / curvature
    direction = lead * right - step_one * first
    merged = step_one * right + step_two * direction
    residual = right - step_one * first - step_two * (lead * first - step_one * second)
    return merged, residual


def solution(mesh):
    in_specs = (P("group", "row", None), P("group", "row", None))
    out_specs = (P(("group", "row"), None), P(("group", "row"), None))
    return jax.shard_map(
        functools.partial(on_device, mesh.shape["row"]),
        mesh=mesh, in_specs=in_specs, out_specs=out_specs, check_vma=False,
    )
```
